32 devices in a mesh: gx: 4 (over z), gy: 2 (over x), gz: 4 (over y, core).
Axes of the slice: x: 2, y: 2, z: 4, core: 2. Of those that a mesh axis runs over, the one named last changes fastest.
Arguments:
- snapshot: bfloat16 [16, 32, 96, 256], P(None, 'gx', 'gz', 'gy'), may hold values from -6 to 6
- factor_two: bfloat16 [256, 128], P('gy'), may hold values from -0.375 to 0.375
- factor_three: bfloat16 [96, 48], P('gz'), may hold values from -0.625 to 0.625
Outputs:
- gram: float32 [32, 32], P('gx', ('gy', 'gz'))
The draws below stay inside these ranges and needn't reach their ends.
All inputs are finite; a program needn't handle non-finite values.
Results may differ from the reference program's by a relative error of at most 0.0003.
Values may be sent and summed in bfloat16 or wider, within the bound.
A program may use at most 64 MiB of HBM per device.

```python
import jax
import jax.numpy as jnp
from jax import lax

S = 16
R2 = 128
R3 = 48
N1 = 32
N2 = 256
N3 = 96


def steps_of(rng, dims, pieces, low, largest):
    loudness, own = 1.0, jax.random.fold_in(rng, 6)
    for dim, blocks in pieces:
        draws = jnp.exp(jax.random.uniform(jax.random.fold_in(own, dim), (blocks,), jnp.float32, low / len(pieces), largest / len(pieces)))
        loudness = loudness * jnp.repeat(draws, dims[dim] // blocks).reshape([-1 if axis == dim else 1 for axis in range(len(dims))])
    return loudness


def noise(key, dims, scale, most, shards=(), kind=jnp.bfloat16):
    loudness = steps_of(key, dims, shards, -0.22, 0.18) if shards else 1.0
    drawn = jax.random.normal(key, dims, jnp.float32) * scale * loudness
    return jnp.minimum(jnp.maximum(drawn, -most), most).astype(kind)


def setup_inputs(seed: int = 0) -> dict:
    keys = jax.random.split(jax.random.key(seed), 4)
    return {
        "snapshot": noise(keys[0], (S, N1, N3, N2), 1.0, 6.0, ((1, 4), (2, 4), (3, 2))),
        "factor_two": noise(keys[1], (N2, R2), N2 ** -0.5, 0.375, ((0, 2),)),
        "factor_three": noise(keys[2], (N3, R3), N3 ** -0.5, 0.625, ((0, 4),)),
    }


def reference(snapshot, factor_two, factor_three):
    projected_three = jnp.einsum("sikj,kr->rsij", snapshot.astype(jnp.float32), factor_three.astype(jnp.float32), precision=lax.Precision.HIGHEST)
    projected_two = jnp.einsum("rsij,jq->qrsi", projected_three, factor_two.astype(jnp.float32), precision=lax.Precision.HIGHEST).astype(jnp.bfloat16)
    flat = projected_two.reshape((R2 * R3 * S, N1))
    gram = jnp.dot(flat.T, flat, preferred_element_type=jnp.float32)
    return gram / float(R2 * R3 * S)
```

```python
import functools

import jax
import jax.numpy as jnp
from jax import lax
from jax.experimental import pallas as pl
from jax.experimental.pallas import tpu as pltpu
from jax.sharding import PartitionSpec as P

MESH = pl.DeviceIdType.MESH
NT = (((1,), (1,)), ((), ()))


def kernel(dims, snap, f2, f3, out, rx, f2rx, f3own, f3rx, mix, z32, tx2, rx2, g, rx3, h, rx4,
           local_sem, send1, recv1, sendf2, recvf2, sendf3, recvf3, send2, recv2, send3, recv3, send4, recv4):
    GX, GY, GZ, S, C, H, NI, K, R3, N1, total = dims
    G = GY * GZ
    x, y, z = lax.axis_index("gx"), lax.axis_index("gy"), lax.axis_index("gz")
    me = y * GZ + z

    def plane(p):
        return {"gy": lax.div(p, GZ), "gz": lax.rem(p, GZ)}

    def plus(index, offset, size):
        return lax.rem(index + offset, size)

    def species(p, c):
        return lax.div(p, H) * C + c

    def remote(src, dst, send, recv, device):
        return pltpu.make_async_remote_copy(
            src_ref=src, dst_ref=dst, send_sem=send, recv_sem=recv, device_id=device, device_id_type=MESH)

    barrier = pltpu.get_barrier_semaphore()
    for o in range(1, G):
        pl.semaphore_signal(barrier, inc=1, device_id=plane(plus(me, o, G)), device_id_type=MESH)
    for o in range(1, GX):
        pl.semaphore_signal(barrier, inc=1, device_id={"gx": plus(x, o, GX)}, device_id_type=MESH)
    f3own[...] = f3[...].astype(jnp.float32)
    f3rx[z] = f3own[...]
    g[...] = jnp.zeros_like(g)
    own = [pltpu.make_async_copy(snap.at[species(me, c)], rx.at[c, me], local_sem.at[c]) for c in range(C)]
    own.append(pltpu.make_async_copy(f2, f2rx.at[y], local_sem.at[C]))
    for copy in own:
        copy.start()
    pl.semaphore_wait(barrier, G - 1 + GX - 1)

    sends = []
    for o in range(1, GY):
        sends.append(remote(f2, f2rx.at[y], sendf2.at[o], recvf2.at[o], {"gy": plus(y, o, GY)}))
    for o in range(1, GZ):
        sends.append(remote(f3own, f3rx.at[z], sendf3.at[o], recvf3.at[o], {"gz": plus(z, o, GZ)}))
    for c in range(C):
        for o in range(1, G):
            p = plus(me, o, G)
            sends.append(remote(snap.at[species(p, c)], rx.at[c, me], send1.at[c, o], recv1.at[c, o], plane(p)))
    for copy in sends:
        copy.start()

    for o in range(1, GY):
        q = plus(y, GY - o, GY)
        remote(f2, f2rx.at[q], sendf2.at[o], recvf2.at[o], {"gy": q}).wait_recv()
    own[C].wait()
    for o in range(1, GZ):
        q = plus(z, GZ - o, GZ)
        remote(f3own, f3rx.at[q], sendf3.at[o], recvf3.at[o], {"gz": q}).wait_recv()
    whole2 = jnp.concatenate([f2rx[b] for b in range(GY)], axis=0)
    if H > 1:
        R2 = whole2.shape[1]
        lanes = lax.div(lax.broadcasted_iota(jnp.int32, whole2.shape, 1), R2 // H)
        whole2 = jnp.where(lanes == lax.rem(me, H), whole2.astype(jnp.float32), 0.0).astype(jnp.bfloat16)
    whole3 = jnp.concatenate([f3rx[b] for b in range(GZ)] * 2, axis=0).astype(jnp.bfloat16)
    rows = lax.broadcasted_iota(jnp.int32, (R3, R3), 0)
    cols = lax.broadcasted_iota(jnp.int32, (R3, R3), 1)
    unit = jnp.where(rows == cols, 1.0, 0.0).astype(jnp.bfloat16)
    mix[...] = lax.dot_general(unit, whole3, NT, preferred_element_type=jnp.float32).astype(jnp.bfloat16)

    for c in range(C):
        own[c].wait()
        for o in range(1, G):
            p = plus(me, G - o, G)
            remote(snap.at[0], rx.at[c, p], send1.at[c, o], recv1.at[c, o], plane(p)).wait_recv()
        second = []
        for b in range(GZ):
            cells = jnp.concatenate([rx[c, a * GZ + b] for a in range(GY)], axis=1)
            second.append(jnp.dot(cells, whole2, preferred_element_type=jnp.float32))
        for i in range(0, NI, 2):
            pair = []
            for n in (i, i + 1):
                fibre = jnp.concatenate([block[n * K:(n + 1) * K] for block in second], axis=0)
                high = fibre.astype(jnp.bfloat16)
                low = (fibre - high.astype(jnp.float32)).astype(jnp.bfloat16)
                pair.append(jnp.concatenate([high, low], axis=0))
            both = jnp.dot(mix[...], jnp.concatenate(pair, axis=1), preferred_element_type=jnp.float32)
            R2 = both.shape[1] // 2
            z32[c, pl.ds(i, R3, stride=NI), :] = both[:, :R2]
            z32[c, pl.ds(i + 1, R3, stride=NI), :] = both[:, R2:]
        share = R3 // GX * NI
        for b in range(GX):
            tx2[c, b] = z32[c, b * share:(b + 1) * share, :].astype(jnp.bfloat16)
        for o in range(1, GX):
            q = plus(x, o, GX)
            copy = remote(tx2.at[c, q], rx2.at[c, x], send2.at[c, o], recv2.at[c, o], {"gx": q})
            copy.start()
            sends.append(copy)
        rx2[c, x] = tx2[c, x]

    gram = None
    for c in range(C):
        for o in range(1, GX):
            q = plus(x, GX - o, GX)
            remote(tx2.at[c, q], rx2.at[c, q], send2.at[c, o], recv2.at[c, o], {"gx": q}).wait_recv()
        blocks = [rx2[c, b].astype(jnp.float32) for b in range(GX)]
        fibres = jnp.concatenate(
            [jnp.concatenate([block[r * NI:(r + 1) * NI] for block in blocks], axis=0) for r in range(R3 // GX)],
            axis=1).astype(jnp.bfloat16)
        term = lax.dot_general(fibres, fibres, NT, preferred_element_type=jnp.float32)
        gram = term if gram is None else gram + term

    for b in range(GX):
        g[b, :, :N1] = gram[b * NI:(b + 1) * NI]
    for o in range(1, GX):
        q = plus(x, o, GX)
        copy = remote(g.at[q], rx3.at[x], send3.at[o], recv3.at[o], {"gx": q})
        copy.start()
        sends.append(copy)
    rx3[x] = g[x]
    for o in range(1, GX):
        q = plus(x, GX - o, GX)
        remote(g.at[q], rx3.at[q], send3.at[o], recv3.at[o], {"gx": q}).wait_recv()
    h[...] = jnp.sum(rx3[...], axis=0)
    for o in range(1, G):
        copy = remote(h, rx4.at[me], send4.at[o], recv4.at[o], plane(plus(me, o, G)))
        copy.start()
        sends.append(copy)
    rx4[me] = h[...]
    for o in range(1, G):
        p = plus(me, G - o, G)
        remote(h, rx4.at[p], send4.at[o], recv4.at[o], plane(p)).wait_recv()
    summed = jnp.sum(rx4[...], axis=0)
    width = out.shape[1]
    lanes = summed.shape[1]
    summed = pltpu.roll(summed, lax.rem(lanes - width * me, lanes), 1)
    out[...] = summed[:, :width] / total
    for copy in sends:
        copy.wait_send()


def solution(mesh):
    GX, GY, GZ = (mesh.shape[name] for name in ("gx", "gy", "gz"))
    G = GY * GZ

    def per_device(snapshot, factor_two, factor_three):
        S, NI, K, J = snapshot.shape
        R2, R3 = factor_two.shape[1], factor_three.shape[1]
        N1 = NI * GX
        C, H = max(1, S // G), max(1, G // S)
        share = R3 // GX * NI
        lanes = -(-N1 // 128) * 128
        dims = (GX, GY, GZ, S, C, H, NI, K, R3, N1, float(R2 * R3 * S))
        dma = pltpu.SemaphoreType.DMA
        f32, bf16 = jnp.float32, jnp.bfloat16
        return pl.pallas_call(
            functools.partial(kernel, dims),
            out_shape=jax.ShapeDtypeStruct((NI, N1 // G), f32),
            in_specs=[pl.BlockSpec(memory_space=pl.ANY), pl.BlockSpec(memory_space=pl.ANY),
                      pl.BlockSpec(memory_space=pltpu.VMEM)],
            out_specs=pl.BlockSpec(memory_space=pltpu.VMEM),
            scratch_shapes=[
                pltpu.VMEM((C, G, NI * K, J), bf16),
                pltpu.VMEM((GY, J, R2), bf16),
                pltpu.VMEM((K, R3), f32),
                pltpu.VMEM((GZ, K, R3), f32),
                pltpu.VMEM((R3, 2 * GZ * K), bf16),
                pltpu.VMEM((C, R3 * NI, R2), f32),
                pltpu.VMEM((C, GX, share, R2), bf16),
                pltpu.VMEM((C, GX, share, R2), bf16),
                pltpu.VMEM((GX, NI, lanes), f32),
                pltpu.VMEM((GX, NI, lanes), f32),
                pltpu.VMEM((NI, lanes), f32),
                pltpu.VMEM((G, NI, lanes), f32),
                dma((C + 1,)),
                dma((C, G)), dma((C, G)),
                dma((GY,)), dma((GY,)),
                dma((GZ,)), dma((GZ,)),
                dma((C, GX)), dma((C, GX)),
                dma((GX,)), dma((GX,)),
                dma((G,)), dma((G,)),
            ],
            compiler_params=pltpu.CompilerParams(
                collective_id=0, has_side_effects=True, vmem_limit_bytes=32 * 1024 * 1024),
        )(snapshot.reshape(S, NI * K, J), factor_two, factor_three)

    placed = (P(None, "gx", "gz", "gy"), P("gy", None), P("gz", None))
    return jax.shard_map(
        per_device, mesh=mesh, in_specs=placed, out_specs=P("gx", ("gy", "gz")), check_vma=False
    )
```

```python
import functools

import jax
import jax.numpy as jnp
from jax import lax
from jax.experimental import pallas as pl
from jax.experimental.pallas import tpu as pltpu
from jax.sharding import PartitionSpec as P

MESH = pl.DeviceIdType.MESH
NT = (((1,), (1,)), ((), ()))


def kernel(dims, snap, f2, f3, out, rx, f2rx, f3raw, f3own, f3rx, mix, z32, tx2, rx2, g, rx4,
           local_sem, send1, recv1, sendf2, recvf2, sendf3, recvf3, send2, recv2, send4, recv4, line):
    GX, GY, GZ, S, C, D, H, NI, K, R3, N1, total = dims
    G = GY * GZ
    T, NI_, W = C * D, NI // D, N1 // G
    x, y, z = lax.axis_index("gx"), lax.axis_index("gy"), lax.axis_index("gz")
    me = y * GZ + z

    def plane(p):
        return {"gy": lax.div(p, GZ), "gz": lax.rem(p, GZ)}

    def plus(index, offset, size):
        return lax.rem(index + offset, size)

    def cells(p, t):
        return snap.at[lax.div(p, H) * C + t // D, pl.ds(t % D * NI_ * K, NI_ * K)]

    def remote(src, dst, send, recv, device):
        return pltpu.make_async_remote_copy(
            src_ref=src, dst_ref=dst, send_sem=send, recv_sem=recv, device_id=device, device_id_type=MESH)

    barrier = pltpu.get_barrier_semaphore()
    for o in range(1, G):
        pl.semaphore_signal(barrier, inc=1, device_id=plane(plus(me, o, G)), device_id_type=MESH)
    def neighbours(semaphore):
        @pl.when(x > 0)
        def _():
            pl.semaphore_signal(semaphore, inc=1, device_id={"gx": x - 1}, device_id_type=MESH)

        @pl.when(x < GX - 1)
        def _():
            pl.semaphore_signal(semaphore, inc=1, device_id={"gx": x + 1}, device_id_type=MESH)

    beside = jnp.where(x > 0, 1, 0) + jnp.where(x < GX - 1, 1, 0)
    neighbours(barrier)
    first = pltpu.make_async_copy(f3, f3raw, local_sem.at[T + 1])
    first.start()
    own = [pltpu.make_async_copy(cells(me, t), rx.at[t, me], local_sem.at[t]) for t in range(T)]
    own.append(pltpu.make_async_copy(f2, f2rx.at[y], local_sem.at[T]))
    for copy in own:
        copy.start()
    first.wait()
    f3own[...] = f3raw[...].astype(jnp.float32)
    f3rx[z] = f3own[...]
    g[...] = jnp.zeros_like(g)
    pl.semaphore_wait(barrier, G - 1 + beside)

    sends = []
    for o in range(1, GY):
        sends.append(remote(f2, f2rx.at[y], sendf2.at[o], recvf2.at[o], {"gy": plus(y, o, GY)}))
    for o in range(1, GZ):
        sends.append(remote(f3own, f3rx.at[z], sendf3.at[o], recvf3.at[o], {"gz": plus(z, o, GZ)}))
    for t in range(T):
        for o in range(1, G):
            p = plus(me, o, G)
            sends.append(remote(cells(p, t), rx.at[t, me], send1.at[t, o], recv1.at[t, o], plane(p)))
    for copy in sends:
        copy.start()

    for step in range(GX - 2):
        neighbours(line.at[step])
        pl.semaphore_wait(line.at[step], beside)

    for o in range(1, GY):
        q = plus(y, GY - o, GY)
        remote(f2, f2rx.at[q], sendf2.at[o], recvf2.at[o], {"gy": q}).wait_recv()
    own[T].wait()
    for o in range(1, GZ):
        q = plus(z, GZ - o, GZ)
        remote(f3own, f3rx.at[q], sendf3.at[o], recvf3.at[o], {"gz": q}).wait_recv()
    whole2 = jnp.concatenate([f2rx[b] for b in range(GY)], axis=0)
    if H > 1:
        R2 = whole2.shape[1]
        lanes = lax.div(lax.broadcasted_iota(jnp.int32, whole2.shape, 1), R2 // H)
        whole2 = jnp.where(lanes == lax.rem(me, H), whole2.astype(jnp.float32), 0.0).astype(jnp.bfloat16)
    whole3 = jnp.concatenate([f3rx[b] for b in range(GZ)] * 2, axis=0).astype(jnp.bfloat16)
    rows = lax.broadcasted_iota(jnp.int32, (R3, R3), 0)
    cols = lax.broadcasted_iota(jnp.int32, (R3, R3), 1)
    unit = jnp.where(rows == cols, 1.0, 0.0).astype(jnp.bfloat16)
    mix[...] = lax.dot_general(unit, whole3, NT, preferred_element_type=jnp.float32).astype(jnp.bfloat16)

    for t in range(T):
        own[t].wait()
        for o in range(1, G):
            p = plus(me, G - o, G)
            remote(cells(me, t), rx.at[t, p], send1.at[t, o], recv1.at[t, o], plane(p)).wait_recv()
        second = []
        for b in range(GZ):
            wide = jnp.concatenate([rx[t, a * GZ + b] for a in range(GY)], axis=1)
            second.append(jnp.dot(wide, whole2, preferred_element_type=jnp.float32))
        for i in range(0, NI_, 2):
            pair = []
            for n in (i, i + 1):
                fibre = jnp.concatenate([block[n * K:(n + 1) * K] for block in second], axis=0)
                high = fibre.astype(jnp.bfloat16)
                low = (fibre - high.astype(jnp.float32)).astype(jnp.bfloat16)
                pair.append(jnp.concatenate([high, low], axis=0))
            both = jnp.dot(mix[...], jnp.concatenate(pair, axis=1), preferred_element_type=jnp.float32)
            R2 = both.shape[1] // 2
            z32[t, pl.ds(i, R3, stride=NI_), :] = both[:, :R2]
            z32[t, pl.ds(i + 1, R3, stride=NI_), :] = both[:, R2:]
        share = R3 // GX * NI_
        for b in range(GX):
            tx2[t, b] = z32[t, b * share:(b + 1) * share, :].astype(jnp.bfloat16)
        for o in range(1, GX):
            q = plus(x, o, GX)
            copy = remote(tx2.at[t, q], rx2.at[t, x], send2.at[t, o], recv2.at[t, o], {"gx": q})
            copy.start()
            sends.append(copy)
        rx2[t, x] = tx2[t, x]

    gram = None
    for c in range(C):
        for t in range(c * D, c * D + D):
            for o in range(1, GX):
                q = plus(x, GX - o, GX)
                remote(tx2.at[t, q], rx2.at[t, q], send2.at[t, o], recv2.at[t, o], {"gx": q}).wait_recv()
        blocks = [rx2[c * D + d, b].astype(jnp.float32) for b in range(GX) for d in range(D)]
        fibres = jnp.concatenate(
            [jnp.concatenate([block[r * NI_:(r + 1) * NI_] for block in blocks], axis=0) for r in range(R3 // GX)],
            axis=1).astype(jnp.bfloat16)
        term = lax.dot_general(fibres, fibres, NT, preferred_element_type=jnp.float32)
        gram = term if gram is None else gram + term

    for b in range(G):
        g[b, :, :N1] = gram[b * W:(b + 1) * W]
    flat, N = x * G + me, GX * G
    for o in range(1, N):
        d = lax.rem(flat + o, N)
        dx, dp = lax.div(d, G), lax.rem(d, G)
        copy = remote(g.at[dp], rx4.at[flat], send4.at[o], recv4.at[o], {"gx": dx, **plane(dp)})
        copy.start()
        sends.append(copy)
    rx4[flat] = g[me]
    for o in range(1, N):
        d = lax.rem(flat + N - o, N)
        remote(g.at[0], rx4.at[d], send4.at[o], recv4.at[o], {"gx": lax.div(d, G), **plane(lax.rem(d, G))}).wait_recv()
    summed = jnp.sum(rx4[...], axis=0)
    lanes = summed.shape[1]
    summed = pltpu.roll(summed, lax.rem(lanes - NI * x, lanes), 1)
    out[...] = summed[:, :NI] / total
    for copy in sends:
        copy.wait_send()


def solution(mesh):
    GX, GY, GZ = (mesh.shape[name] for name in ("gx", "gy", "gz"))
    G = GY * GZ

    def per_device(snapshot, factor_two, factor_three):
        S, NI, K, J = snapshot.shape
        R2, R3 = factor_two.shape[1], factor_three.shape[1]
        N1 = NI * GX
        C, H = max(1, S // G), max(1, G // S)
        share = R3 // GX * NI
        lanes = -(-N1 // 128) * 128
        D = 2 if share % 32 == 0 else 1
        part = NI // D
        dims = (GX, GY, GZ, S, C, D, H, NI, K, R3, N1, float(R2 * R3 * S))
        dma = pltpu.SemaphoreType.DMA
        f32, bf16 = jnp.float32, jnp.bfloat16
        return pl.pallas_call(
            functools.partial(kernel, dims),
            out_shape=jax.ShapeDtypeStruct((N1 // G, NI), f32),
            in_specs=[pl.BlockSpec(memory_space=pl.ANY)] * 3,
            out_specs=pl.BlockSpec(memory_space=pltpu.VMEM),
            scratch_shapes=[
                pltpu.VMEM((C * D, G, part * K, J), bf16),
                pltpu.VMEM((GY, J, R2), bf16),
                pltpu.VMEM((K, R3), bf16),
                pltpu.VMEM((K, R3), f32),
                pltpu.VMEM((GZ, K, R3), f32),
                pltpu.VMEM((R3, 2 * GZ * K), bf16),
                pltpu.VMEM((C * D, R3 * part, R2), f32),
                pltpu.VMEM((C * D, GX, share // D, R2), bf16),
                pltpu.VMEM((C * D, GX, share // D, R2), bf16),
                pltpu.VMEM((G, N1 // G, lanes), f32),
                pltpu.VMEM((GX * G, N1 // G, lanes), f32),
                dma((C * D + 2,)),
                dma((C * D, G)), dma((C * D, G)),
                dma((GY,)), dma((GY,)),
                dma((GZ,)), dma((GZ,)),
                dma((C * D, GX)), dma((C * D, GX)),
                dma((GX * G,)), dma((GX * G,)),
                pltpu.SemaphoreType.REGULAR((max(1, GX - 2),)),
            ],
            compiler_params=pltpu.CompilerParams(
                collective_id=0, has_side_effects=True, vmem_limit_bytes=62 * 1024 * 1024),
        )(snapshot.reshape(S, NI * K, J), factor_two, factor_three).T

    placed = (P(None, "gx", "gz", "gy"), P("gy", None), P("gz", None))
    return jax.shard_map(
        per_device, mesh=mesh, in_specs=placed, out_specs=P("gx", ("gy", "gz")), check_vma=False
    )
```

```python
import functools

import jax
import jax.numpy as jnp
from jax import lax
from jax.experimental import pallas as pl
from jax.experimental.pallas import tpu as pltpu
from jax.sharding import PartitionSpec as P

MESH = pl.DeviceIdType.MESH
NT = (((1,), (1,)), ((), ()))


def kernel(dims, snap, f2, f3, out, rx, f2rx, f3raw, f3own, f3rx, mix, z32, tx2, rx2, g, rx4,
           local_sem, send1, recv1, sendf2, recvf2, sendf3, recvf3, send2, recv2, send4, recv4, line):
    GX, GY, GZ, S, C, D, H, NI, K, R3, N1, total = dims
    G = GY * GZ
    T, NI_, W = C * D, NI // D, N1 // G
    x, y, z = lax.axis_index("gx"), lax.axis_index("gy"), lax.axis_index("gz")
    me = y * GZ + z

    def plane(p):
        return {"gy": lax.div(p, GZ), "gz": lax.rem(p, GZ)}

    def plus(index, offset, size):
        return lax.rem(index + offset, size)

    def cells(p, t):
        return snap.at[lax.div(p, H) * C + t // D, pl.ds(t % D * NI_ * K, NI_ * K)]

    def remote(src, dst, send, recv, device):
        return pltpu.make_async_remote_copy(
            src_ref=src, dst_ref=dst, send_sem=send, recv_sem=recv, device_id=device, device_id_type=MESH)

    barrier = pltpu.get_barrier_semaphore()
    for o in range(1, G):
        pl.semaphore_signal(barrier, inc=1, device_id=plane(plus(me, o, G)), device_id_type=MESH)
    def neighbours(semaphore):
        @pl.when(x > 0)
        def _():
            pl.semaphore_signal(semaphore, inc=1, device_id={"gx": x - 1}, device_id_type=MESH)

        @pl.when(x < GX - 1)
        def _():
            pl.semaphore_signal(semaphore, inc=1, device_id={"gx": x + 1}, device_id_type=MESH)

    beside = jnp.where(x > 0, 1, 0) + jnp.where(x < GX - 1, 1, 0)
    neighbours(barrier)
    first = pltpu.make_async_copy(f3, f3raw, local_sem.at[T + 1])
    first.start()
    own = [pltpu.make_async_copy(cells(me, t), rx.at[t, me], local_sem.at[t]) for t in range(T)]
    own.append(pltpu.make_async_copy(f2, f2rx.at[y], local_sem.at[T]))
    for copy in own:
        copy.start()
    first.wait()
    f3own[...] = f3raw[...].astype(jnp.float32)
    f3rx[z] = f3own[...]
    g[...] = jnp.zeros_like(g)
    pl.semaphore_wait(barrier, G - 1 + beside)

    sends = []
    for o in range(1, GY):
        sends.append(remote(f2, f2rx.at[y], sendf2.at[o], recvf2.at[o], {"gy": plus(y, o, GY)}))
    for o in range(1, GZ):
        sends.append(remote(f3own, f3rx.at[z], sendf3.at[o], recvf3.at[o], {"gz": plus(z, o, GZ)}))
    for copy in sends:
        copy.start()
    far = sorted(range(GZ), key=lambda b: -min(b, GZ - b))
    for t in range(T):
        for a, b in [(a, b) for a in reversed(range(GY)) for b in far if a or b]:
            p = plus(y, a, GY) * GZ + plus(z, b, GZ)
            remote(cells(p, t), rx.at[t, me], send1.at[t], recv1.at[t], plane(p)).start()

    for step in range(GX - 2):
        neighbours(line.at[step])
        pl.semaphore_wait(line.at[step], beside)

    for o in range(1, GY):
        q = plus(y, GY - o, GY)
        remote(f2, f2rx.at[q], sendf2.at[o], recvf2.at[o], {"gy": q}).wait_recv()
    own[T].wait()
    for o in range(1, GZ):
        q = plus(z, GZ - o, GZ)
        remote(f3own, f3rx.at[q], sendf3.at[o], recvf3.at[o], {"gz": q}).wait_recv()
    whole2 = jnp.concatenate([f2rx[b] for b in range(GY)], axis=0)
    if H > 1:
        R2 = whole2.shape[1]
        lanes = lax.div(lax.broadcasted_iota(jnp.int32, whole2.shape, 1), R2 // H)
        whole2 = jnp.where(lanes == lax.rem(me, H), whole2.astype(jnp.float32), 0.0).astype(jnp.bfloat16)
    whole3 = jnp.concatenate([f3rx[b] for b in range(GZ)] * 2, axis=0).astype(jnp.bfloat16)
    rows = lax.broadcasted_iota(jnp.int32, (R3, R3), 0)
    cols = lax.broadcasted_iota(jnp.int32, (R3, R3), 1)
    unit = jnp.where(rows == cols, 1.0, 0.0).astype(jnp.bfloat16)
    mix[...] = lax.dot_general(unit, whole3, NT, preferred_element_type=jnp.float32).astype(jnp.bfloat16)

    for t in range(T):
        own[t].wait()
        arrived = rx.at[t, pl.ds(0, G - 1)]
        remote(arrived, arrived, send1.at[t], recv1.at[t], plane(plus(me, 1, G))).wait_recv()
        second = []
        for b in range(GZ):
            wide = jnp.concatenate([rx[t, a * GZ + b] for a in range(GY)], axis=1)
            second.append(jnp.dot(wide, whole2, preferred_element_type=jnp.float32))
        for i in range(0, NI_, 2):
            pair = []
            for n in (i, i + 1):
                fibre = jnp.concatenate([block[n * K:(n + 1) * K] for block in second], axis=0)
                high = fibre.astype(jnp.bfloat16)
                low = (fibre - high.astype(jnp.float32)).astype(jnp.bfloat16)
                pair.append(jnp.concatenate([high, low], axis=0))
            both = jnp.dot(mix[...], jnp.concatenate(pair, axis=1), preferred_element_type=jnp.float32)
            R2 = both.shape[1] // 2
            z32[t, pl.ds(i, R3, stride=NI_), :] = both[:, :R2]
            z32[t, pl.ds(i + 1, R3, stride=NI_), :] = both[:, R2:]
        share = R3 // GX * NI_
        for b in range(GX):
            tx2[t, b] = z32[t, b * share:(b + 1) * share, :].astype(jnp.bfloat16)
        for o in range(1, GX):
            q = plus(x, o, GX)
            copy = remote(tx2.at[t, q], rx2.at[t, x], send2.at[t], recv2.at[t], {"gx": q})
            copy.start()
        rx2[t, x] = tx2[t, x]

    gram = None
    for c in range(C):
        for t in range(c * D, c * D + D):
            gathered = rx2.at[t, pl.ds(0, GX - 1)]
            remote(gathered, gathered, send2.at[t], recv2.at[t], {"gx": plus(x, 1, GX)}).wait_recv()
        blocks = [rx2[c * D + d, b].astype(jnp.float32) for b in range(GX) for d in range(D)]
        fibres = jnp.concatenate(
            [jnp.concatenate([block[r * NI_:(r + 1) * NI_] for block in blocks], axis=0) for r in range(R3 // GX)],
            axis=1).astype(jnp.bfloat16)
        term = lax.dot_general(fibres, fibres, NT, preferred_element_type=jnp.float32)
        gram = term if gram is None else gram + term

    for b in range(G):
        g[b, :, :N1] = gram[b * W:(b + 1) * W]
    flat, N = x * G + me, GX * G
    for o in range(1, N):
        d = lax.rem(flat + o, N)
        dx, dp = lax.div(d, G), lax.rem(d, G)
        copy = remote(g.at[dp], rx4.at[flat], send4.at[0], recv4.at[0], {"gx": dx, **plane(dp)})
        copy.start()
    rx4[flat] = g[me]
    for t in range(T):
        arrived = rx.at[t, pl.ds(0, G - 1)]
        remote(arrived, arrived, send1.at[t], recv1.at[t], plane(plus(me, 1, G))).wait_send()
        gathered = rx2.at[t, pl.ds(0, GX - 1)]
        remote(gathered, gathered, send2.at[t], recv2.at[t], {"gx": plus(x, 1, GX)}).wait_send()
    for copy in sends:
        copy.wait_send()
    others = rx4.at[pl.ds(0, N - 1)]
    remote(others, others, send4.at[0], recv4.at[0], plane(plus(me, 1, G))).wait_recv()
    summed = jnp.sum(rx4[...], axis=0)
    lanes = summed.shape[1]
    summed = pltpu.roll(summed, lax.rem(lanes - NI * x, lanes), 1)
    out[...] = summed[:, :NI] / total
    remote(others, others, send4.at[0], recv4.at[0], plane(plus(me, 1, G))).wait_send()


def solution(mesh):
    GX, GY, GZ = (mesh.shape[name] for name in ("gx", "gy", "gz"))
    G = GY * GZ

    def per_device(snapshot, factor_two, factor_three):
        S, NI, K, J = snapshot.shape
        R2, R3 = factor_two.shape[1], factor_three.shape[1]
        N1 = NI * GX
        C, H = max(1, S // G), max(1, G // S)
        share = R3 // GX * NI
        lanes = -(-N1 // 128) * 128
        D = 2 if share % 32 == 0 else 1
        part = NI // D
        dims = (GX, GY, GZ, S, C, D, H, NI, K, R3, N1, float(R2 * R3 * S))
        dma = pltpu.SemaphoreType.DMA
        f32, bf16 = jnp.float32, jnp.bfloat16
        return pl.pallas_call(
            functools.partial(kernel, dims),
            out_shape=pltpu.VMEM((N1 // G, NI), f32),
            in_specs=[pl.BlockSpec(memory_space=pl.ANY)] * 3,
            out_specs=pl.BlockSpec(memory_space=pltpu.VMEM),
            scratch_shapes=[
                pltpu.VMEM((C * D, G, part * K, J), bf16),
                pltpu.VMEM((GY, J, R2), bf16),
                pltpu.VMEM((K, R3), bf16),
                pltpu.VMEM((K, R3), f32),
                pltpu.VMEM((GZ, K, R3), f32),
                pltpu.VMEM((R3, 2 * GZ * K), bf16),
                pltpu.VMEM((C * D, R3 * part, R2), f32),
                pltpu.VMEM((C * D, GX, share // D, R2), bf16),
                pltpu.VMEM((C * D, GX, share // D, R2), bf16),
                pltpu.VMEM((G, N1 // G, lanes), f32),
                pltpu.VMEM((GX * G, N1 // G, lanes), f32),
                dma((C * D + 2,)),
                dma((C * D,)), dma((C * D,)),
                dma((GY,)), dma((GY,)),
                dma((GZ,)), dma((GZ,)),
                dma((C * D,)), dma((C * D,)),
                dma((1,)), dma((1,)),
                pltpu.SemaphoreType.REGULAR((max(1, GX - 2),)),
            ],
            compiler_params=pltpu.CompilerParams(
                collective_id=0, has_side_effects=True, vmem_limit_bytes=62 * 1024 * 1024),
        )(snapshot.reshape(S, NI * K, J), factor_two, factor_three).T

    placed = (P(None, "gx", "gz", "gy"), P("gy", None), P("gz", None))
    return jax.shard_map(
        per_device, mesh=mesh, in_specs=placed, out_specs=P("gx", ("gy", "gz")), check_vma=False
    )
```

```python
import functools

import jax
import jax.numpy as jnp
from jax import lax
from jax.experimental import pallas as pl
from jax.experimental.pallas import tpu as pltpu
from jax.sharding import PartitionSpec as P

MESH = pl.DeviceIdType.MESH
NT = (((1,), (1,)), ((), ()))


def kernel(dims, snap, f2, f3, out, rx, f2rx, f3raw, f3own, f3rx, mix, z32, tx2, rx2, g, rx4,
           local_sem, send1, recv1, sendf2, recvf2, sendf3, recvf3, send2, recv2, send4, recv4, line):
    GX, GY, GZ, S, C, D, H, NI, K, R3, N1, total = dims
    G = GY * GZ
    T, NI_, W = C * D, NI // D, N1 // G
    x, y, z = lax.axis_index("gx"), lax.axis_index("gy"), lax.axis_index("gz")
    me = y * GZ + z

    def plane(p):
        return {"gy": lax.div(p, GZ), "gz": lax.rem(p, GZ)}

    def plus(index, offset, size):
        return lax.rem(index + offset, size)

    def cells(p, t):
        return snap.at[lax.div(p, H) * C + t // D, pl.ds(t % D * NI_ * K, NI_ * K)]

    def remote(src, dst, send, recv, device):
        return pltpu.make_async_remote_copy(
            src_ref=src, dst_ref=dst, send_sem=send, recv_sem=recv, device_id=device, device_id_type=MESH)

    barrier = pltpu.get_barrier_semaphore()
    for o in range(1, GZ):
        pl.semaphore_signal(barrier, inc=1, device_id={"gz": plus(z, o, GZ)}, device_id_type=MESH)
    for o in range(1, GY):
        pl.semaphore_signal(barrier, inc=1, device_id={"gy": plus(y, o, GY)}, device_id_type=MESH)

    def neighbours(semaphore):
        @pl.when(x > 0)
        def _():
            pl.semaphore_signal(semaphore, inc=1, device_id={"gx": x - 1}, device_id_type=MESH)

        @pl.when(x < GX - 1)
        def _():
            pl.semaphore_signal(semaphore, inc=1, device_id={"gx": x + 1}, device_id_type=MESH)

    beside = jnp.where(x > 0, 1, 0) + jnp.where(x < GX - 1, 1, 0)
    neighbours(barrier)
    first = pltpu.make_async_copy(f3, f3raw, local_sem.at[T + 1])
    first.start()
    own = [pltpu.make_async_copy(cells(me, t), rx.at[t, me], local_sem.at[t]) for t in range(T)]
    own.append(pltpu.make_async_copy(f2, f2rx.at[y], local_sem.at[T]))
    for copy in own:
        copy.start()
    pl.semaphore_wait(barrier, GY - 1 + GZ - 1 + beside)

    far = sorted(range(GZ), key=lambda b: -min(b, GZ - b))

    near = [(0, b) for b in far if b] + [(a, 0) for a in range(1, GY)]
    cross = [(a, b) for a in reversed(range(1, GY)) for b in far if b]

    def spread(t, offsets):
        for a, b in offsets:
            place = {"gy": plus(y, a, GY), "gz": plus(z, b, GZ)}
            p = place["gy"] * GZ + place["gz"]
            remote(cells(p, t), rx.at[t, me], send1.at[t], recv1.at[t], place).start()

    for o in range(1, GY):
        pl.semaphore_signal(line.at[GX - 2], inc=1, device_id={"gy": plus(y, o, GY)}, device_id_type=MESH)
    spread(0, near)
    pl.semaphore_wait(line.at[GX - 2], GY - 1)
    spread(0, cross)
    first.wait()
    f3own[...] = f3raw[...].astype(jnp.float32)
    sends = []
    for o in range(1, GZ):
        sends.append(remote(f3own, f3rx.at[z], sendf3.at[o], recvf3.at[o], {"gz": plus(z, o, GZ)}))
    for o in range(1, GY):
        sends.append(remote(f2, f2rx.at[y], sendf2.at[o], recvf2.at[o], {"gy": plus(y, o, GY)}))
    for copy in sends:
        copy.start()
    for t in range(1, T):
        spread(t, cross + near)
    f3rx[z] = f3own[...]
    g[...] = jnp.zeros_like(g)

    for step in range(GX - 2):
        neighbours(line.at[step])
        pl.semaphore_wait(line.at[step], beside)

    for o in range(1, GY):
        q = plus(y, GY - o, GY)
        remote(f2, f2rx.at[q], sendf2.at[o], recvf2.at[o], {"gy": q}).wait_recv()
    own[T].wait()
    for o in range(1, GZ):
        q = plus(z, GZ - o, GZ)
        remote(f3own, f3rx.at[q], sendf3.at[o], recvf3.at[o], {"gz": q}).wait_recv()
    whole2 = jnp.concatenate([f2rx[b] for b in range(GY)], axis=0)
    if H > 1:
        R2 = whole2.shape[1]
        lanes = lax.div(lax.broadcasted_iota(jnp.int32, whole2.shape, 1), R2 // H)
        whole2 = jnp.where(lanes == lax.rem(me, H), whole2.astype(jnp.float32), 0.0).astype(jnp.bfloat16)
    whole3 = jnp.concatenate([f3rx[b] for b in range(GZ)] * 2, axis=0).astype(jnp.bfloat16)
    rows = lax.broadcasted_iota(jnp.int32, (R3, R3), 0)
    cols = lax.broadcasted_iota(jnp.int32, (R3, R3), 1)
    unit = jnp.where(rows == cols, 1.0, 0.0).astype(jnp.bfloat16)
    mix[...] = lax.dot_general(unit, whole3, NT, preferred_element_type=jnp.float32).astype(jnp.bfloat16)

    for t in range(T):
        own[t].wait()
        arrived = rx.at[t, pl.ds(0, G - 1)]
        remote(arrived, arrived, send1.at[t], recv1.at[t], plane(plus(me, 1, G))).wait_recv()
        second = []
        for b in range(GZ):
            wide = jnp.concatenate([rx[t, a * GZ + b] for a in range(GY)], axis=1)
            second.append(jnp.dot(wide, whole2, preferred_element_type=jnp.float32))
        for i in range(0, NI_, 2):
            pair = []
            for n in (i, i + 1):
                fibre = jnp.concatenate([block[n * K:(n + 1) * K] for block in second], axis=0)
                high = fibre.astype(jnp.bfloat16)
                low = (fibre - high.astype(jnp.float32)).astype(jnp.bfloat16)
                pair.append(jnp.concatenate([high, low], axis=0))
            both = jnp.dot(mix[...], jnp.concatenate(pair, axis=1), preferred_element_type=jnp.float32)
            R2 = both.shape[1] // 2
            z32[t, pl.ds(i, R3, stride=NI_), :] = both[:, :R2]
            z32[t, pl.ds(i + 1, R3, stride=NI_), :] = both[:, R2:]
        share = R3 // GX * NI_
        for b in range(GX):
            tx2[t, b] = z32[t, b * share:(b + 1) * share, :].astype(jnp.bfloat16)
        for o in range(1, GX):
            q = plus(x, o, GX)
            copy = remote(tx2.at[t, q], rx2.at[t, x], send2.at[t], recv2.at[t], {"gx": q})
            copy.start()
        rx2[t, x] = tx2[t, x]

    gram = None
    for c in range(C):
        for t in range(c * D, c * D + D):
            gathered = rx2.at[t, pl.ds(0, GX - 1)]
            remote(gathered, gathered, send2.at[t], recv2.at[t], {"gx": plus(x, 1, GX)}).wait_recv()
        blocks = [rx2[c * D + d, b].astype(jnp.float32) for b in range(GX) for d in range(D)]
        fibres = jnp.concatenate(
            [jnp.concatenate([block[r * NI_:(r + 1) * NI_] for block in blocks], axis=0) for r in range(R3 // GX)],
            axis=1).astype(jnp.bfloat16)
        term = lax.dot_general(fibres, fibres, NT, preferred_element_type=jnp.float32)
        gram = term if gram is None else gram + term

    for b in range(G):
        g[b, :, :N1] = gram[b * W:(b + 1) * W]
    flat, N = x * G + me, GX * G
    columns = [plus(me, b, G) for b in range(G)]
    places = [plane(p) for p in columns]
    for a in range(GX):
        dx = plus(x, a, GX)
        for b in range(1 if a == 0 else 0, G):
            remote(g.at[columns[b]], rx4.at[flat], send4.at[0], recv4.at[0], {"gx": dx, **places[b]}).start()
    rx4[flat] = g[me]
    for t in range(T):
        arrived = rx.at[t, pl.ds(0, G - 1)]
        remote(arrived, arrived, send1.at[t], recv1.at[t], plane(plus(me, 1, G))).wait_send()
        gathered = rx2.at[t, pl.ds(0, GX - 1)]
        remote(gathered, gathered, send2.at[t], recv2.at[t], {"gx": plus(x, 1, GX)}).wait_send()
    for copy in sends:
        copy.wait_send()
    others = rx4.at[pl.ds(0, N - 1)]
    remote(others, others, send4.at[0], recv4.at[0], plane(plus(me, 1, G))).wait_recv()
    summed = jnp.sum(rx4[...], axis=0)
    lanes = summed.shape[1]
    summed = pltpu.roll(summed, lax.rem(lanes - NI * x, lanes), 1)
    out[...] = summed[:, :NI] / total
    remote(others, others, send4.at[0], recv4.at[0], plane(plus(me, 1, G))).wait_send()


def solution(mesh):
    GX, GY, GZ = (mesh.shape[name] for name in ("gx", "gy", "gz"))
    G = GY * GZ

    def per_device(snapshot, factor_two, factor_three):
        S, NI, K, J = snapshot.shape
        R2, R3 = factor_two.shape[1], factor_three.shape[1]
        N1 = NI * GX
        C, H = max(1, S // G), max(1, G // S)
        share = R3 // GX * NI
        lanes = -(-N1 // 128) * 128
        D = 2 if share % 32 == 0 else 1
        part = NI // D
        dims = (GX, GY, GZ, S, C, D, H, NI, K, R3, N1, float(R2 * R3 * S))
        dma = pltpu.SemaphoreType.DMA
        f32, bf16 = jnp.float32, jnp.bfloat16
        return pl.pallas_call(
            functools.partial(kernel, dims),
            out_shape=pltpu.VMEM((N1 // G, NI), f32),
            in_specs=[pl.BlockSpec(memory_space=pl.ANY)] * 3,
            out_specs=pl.BlockSpec(memory_space=pltpu.VMEM),
            scratch_shapes=[
                pltpu.VMEM((C * D, G, part * K, J), bf16),
                pltpu.VMEM((GY, J, R2), bf16),
                pltpu.VMEM((K, R3), bf16),
                pltpu.VMEM((K, R3), f32),
                pltpu.VMEM((GZ, K, R3), f32),
                pltpu.VMEM((R3, 2 * GZ * K), bf16),
                pltpu.VMEM((C * D, R3 * part, R2), f32),
                pltpu.VMEM((C * D, GX, share // D, R2), bf16),
                pltpu.VMEM((C * D, GX, share // D, R2), bf16),
                pltpu.VMEM((G, N1 // G, lanes), f32),
                pltpu.VMEM((GX * G, N1 // G, lanes), f32),
                dma((C * D + 2,)),
                dma((C * D,)), dma((C * D,)),
                dma((GY,)), dma((GY,)),
                dma((GZ,)), dma((GZ,)),
                dma((C * D,)), dma((C * D,)),
                dma((1,)), dma((1,)),
                pltpu.SemaphoreType.REGULAR((GX - 1,)),
            ],
            compiler_params=pltpu.CompilerParams(
                collective_id=0, has_side_effects=True, vmem_limit_bytes=62 * 1024 * 1024),
        )(snapshot.reshape(S, NI * K, J), factor_two, factor_three).T

    placed = (P(None, "gx", "gz", "gy"), P("gy", None), P("gz", None))
    return jax.shard_map(
        per_device, mesh=mesh, in_specs=placed, out_specs=P("gx", ("gy", "gz")), check_vma=False
    )
```

```python
import functools

import jax
import jax.numpy as jnp
from jax import lax
from jax.experimental import pallas as pl
from jax.experimental.pallas import tpu as pltpu
from jax.sharding import PartitionSpec as P

MESH = pl.DeviceIdType.MESH
NT = (((1,), (1,)), ((), ()))


def kernel(dims, snap, f2, f3, out, rx, f2rx, f3raw, f3own, f3rx, mix, z32, tx2, rx2, g, rx4,
           local_sem, send1, recv1, sendf2, recvf2, sendf3, recvf3, send2, recv2, send4, recv4, line):
    GX, GY, GZ, S, C, D, H, NI, K, R3, N1, total = dims
    G = GY * GZ
    T, NI_, W = C * D, NI // D, N1 // G
    x, y, z = lax.axis_index("gx"), lax.axis_index("gy"), lax.axis_index("gz")
    me = y * GZ + z

    def plane(p):
        return {"gy": lax.div(p, GZ), "gz": lax.rem(p, GZ)}

    def plus(index, offset, size):
        return lax.rem(index + offset, size)

    def cells(p, t):
        return snap.at[lax.div(p, H) * C + t // D, pl.ds(t % D * NI_ * K, NI_ * K)]

    def remote(src, dst, send, recv, device):
        return pltpu.make_async_remote_copy(
            src_ref=src, dst_ref=dst, send_sem=send, recv_sem=recv, device_id=device, device_id_type=MESH)

    barrier = pltpu.get_barrier_semaphore()
    for o in range(1, GZ):
        pl.semaphore_signal(barrier, inc=1, device_id={"gz": plus(z, o, GZ)}, device_id_type=MESH)
    for o in range(1, GY):
        pl.semaphore_signal(barrier, inc=1, device_id={"gy": plus(y, o, GY)}, device_id_type=MESH)

    def neighbours(semaphore):
        @pl.when(x > 0)
        def _():
            pl.semaphore_signal(semaphore, inc=1, device_id={"gx": x - 1}, device_id_type=MESH)

        @pl.when(x < GX - 1)
        def _():
            pl.semaphore_signal(semaphore, inc=1, device_id={"gx": x + 1}, device_id_type=MESH)

    beside = jnp.where(x > 0, 1, 0) + jnp.where(x < GX - 1, 1, 0)
    neighbours(barrier)
    first = pltpu.make_async_copy(f3, f3raw, local_sem.at[T + 1])
    first.start()
    own = [pltpu.make_async_copy(cells(me, t), rx.at[t, me], local_sem.at[t]) for t in range(T)]
    own.append(pltpu.make_async_copy(f2, f2rx.at[y], local_sem.at[T]))
    for copy in own:
        copy.start()
    pl.semaphore_wait(barrier, GY - 1 + GZ - 1 + beside)

    far = sorted(range(GZ), key=lambda b: -min(b, GZ - b))

    near = [(0, b) for b in far if b] + [(a, 0) for a in range(1, GY)]
    cross = [(a, b) for a in reversed(range(1, GY)) for b in far if b]

    def spread(t, offsets):
        for a, b in offsets:
            place = {"gy": plus(y, a, GY), "gz": plus(z, b, GZ)}
            p = place["gy"] * GZ + place["gz"]
            remote(cells(p, t), rx.at[t, me], send1.at[t], recv1.at[t], place).start()

    for o in range(1, GY):
        pl.semaphore_signal(line.at[GX - 2], inc=1, device_id={"gy": plus(y, o, GY)}, device_id_type=MESH)
    early = [remote(f2, f2rx.at[y], sendf2.at[o], recvf2.at[o], {"gy": plus(y, o, GY)}) for o in range(1, GY)]
    for copy in early:
        copy.start()
    spread(0, near)
    pl.semaphore_wait(line.at[GX - 2], GY - 1)
    spread(0, cross)
    first.wait()
    f3own[...] = f3raw[...].astype(jnp.float32)
    sends = []
    for o in range(1, GZ):
        sends.append(remote(f3own, f3rx.at[z], sendf3.at[o], recvf3.at[o], {"gz": plus(z, o, GZ)}))
    for copy in sends:
        copy.start()
    sends.extend(early)
    for t in range(1, T):
        spread(t, cross + near)
    f3rx[z] = f3own[...]
    g[...] = jnp.zeros_like(g)

    for step in range(GX - 2):
        neighbours(line.at[step])
        pl.semaphore_wait(line.at[step], beside)

    for o in range(1, GY):
        q = plus(y, GY - o, GY)
        remote(f2, f2rx.at[q], sendf2.at[o], recvf2.at[o], {"gy": q}).wait_recv()
    own[T].wait()
    for o in range(1, GZ):
        q = plus(z, GZ - o, GZ)
        remote(f3own, f3rx.at[q], sendf3.at[o], recvf3.at[o], {"gz": q}).wait_recv()
    whole2 = jnp.concatenate([f2rx[b] for b in range(GY)], axis=0)
    if H > 1:
        R2 = whole2.shape[1]
        lanes = lax.div(lax.broadcasted_iota(jnp.int32, whole2.shape, 1), R2 // H)
        whole2 = jnp.where(lanes == lax.rem(me, H), whole2.astype(jnp.float32), 0.0).astype(jnp.bfloat16)
    whole3 = jnp.concatenate([f3rx[b] for b in range(GZ)] * 2, axis=0).astype(jnp.bfloat16)
    rows = lax.broadcasted_iota(jnp.int32, (R3, R3), 0)
    cols = lax.broadcasted_iota(jnp.int32, (R3, R3), 1)
    unit = jnp.where(rows == cols, 1.0, 0.0).astype(jnp.bfloat16)
    mix[...] = lax.dot_general(unit, whole3, NT, preferred_element_type=jnp.float32).astype(jnp.bfloat16)

    for t in range(T):
        own[t].wait()
        arrived = rx.at[t, pl.ds(0, G - 1)]
        remote(arrived, arrived, send1.at[t], recv1.at[t], plane(plus(me, 1, G))).wait_recv()
        second = []
        for b in range(GZ):
            wide = jnp.concatenate([rx[t, a * GZ + b] for a in range(GY)], axis=1)
            second.append(jnp.dot(wide, whole2, preferred_element_type=jnp.float32))
        for i in range(0, NI_, 2):
            pair = []
            for n in (i, i + 1):
                fibre = jnp.concatenate([block[n * K:(n + 1) * K] for block in second], axis=0)
                high = fibre.astype(jnp.bfloat16)
                low = (fibre - high.astype(jnp.float32)).astype(jnp.bfloat16)
                pair.append(jnp.concatenate([high, low], axis=0))
            both = jnp.dot(mix[...], jnp.concatenate(pair, axis=1), preferred_element_type=jnp.float32)
            R2 = both.shape[1] // 2
            z32[t, pl.ds(i, R3, stride=NI_), :] = both[:, :R2]
            z32[t, pl.ds(i + 1, R3, stride=NI_), :] = both[:, R2:]
        share = R3 // GX * NI_
        for b in range(GX):
            tx2[t, b] = z32[t, b * share:(b + 1) * share, :].astype(jnp.bfloat16)
        for o in range(1, GX):
            q = plus(x, o, GX)
            copy = remote(tx2.at[t, q], rx2.at[t, x], send2.at[t], recv2.at[t], {"gx": q})
            copy.start()
        rx2[t, x] = tx2[t, x]

    gram = None
    for c in range(C):
        for t in range(c * D, c * D + D):
            gathered = rx2.at[t, pl.ds(0, GX - 1)]
            remote(gathered, gathered, send2.at[t], recv2.at[t], {"gx": plus(x, 1, GX)}).wait_recv()
        blocks = [rx2[c * D + d, b].astype(jnp.float32) for b in range(GX) for d in range(D)]
        fibres = jnp.concatenate(
            [jnp.concatenate([block[r * NI_:(r + 1) * NI_] for block in blocks], axis=0) for r in range(R3 // GX)],
            axis=1).astype(jnp.bfloat16)
        term = lax.dot_general(fibres, fibres, NT, preferred_element_type=jnp.float32)
        gram = term if gram is None else gram + term

    for b in range(G):
        g[b, :, :N1] = gram[b * W:(b + 1) * W]
    flat, N = x * G + me, GX * G
    columns = [plus(me, b, G) for b in range(G)]
    places = [plane(p) for p in columns]
    for a in range(GX):
        dx = plus(x, a, GX)
        for b in range(1 if a == 0 else 0, G):
            remote(g.at[columns[b]], rx4.at[flat], send4.at[0], recv4.at[0], {"gx": dx, **places[b]}).start()
    rx4[flat] = g[me]
    for t in range(T):
        arrived = rx.at[t, pl.ds(0, G - 1)]
        remote(arrived, arrived, send1.at[t], recv1.at[t], plane(plus(me, 1, G))).wait_send()
        gathered = rx2.at[t, pl.ds(0, GX - 1)]
        remote(gathered, gathered, send2.at[t], recv2.at[t], {"gx": plus(x, 1, GX)}).wait_send()
    for copy in sends:
        copy.wait_send()
    others = rx4.at[pl.ds(0, N - 1)]
    remote(others, others, send4.at[0], recv4.at[0], plane(plus(me, 1, G))).wait_recv()
    summed = jnp.sum(rx4[...], axis=0)
    lanes = summed.shape[1]
    summed = pltpu.roll(summed, lax.rem(lanes - NI * x, lanes), 1)
    out[...] = summed[:, :NI] / total
    remote(others, others, send4.at[0], recv4.at[0], plane(plus(me, 1, G))).wait_send()


def solution(mesh):
    GX, GY, GZ = (mesh.shape[name] for name in ("gx", "gy", "gz"))
    G = GY * GZ

    def per_device(snapshot, factor_two, factor_three):
        S, NI, K, J = snapshot.shape
        R2, R3 = factor_two.shape[1], factor_three.shape[1]
        N1 = NI * GX
        C, H = max(1, S // G), max(1, G // S)
        share = R3 // GX * NI
        lanes = -(-N1 // 128) * 128
        D = 2 if share % 32 == 0 else 1
        part = NI // D
        dims = (GX, GY, GZ, S, C, D, H, NI, K, R3, N1, float(R2 * R3 * S))
        dma = pltpu.SemaphoreType.DMA
        f32, bf16 = jnp.float32, jnp.bfloat16
        return pl.pallas_call(
            functools.partial(kernel, dims),
            out_shape=pltpu.VMEM((N1 // G, NI), f32),
            in_specs=[pl.BlockSpec(memory_space=pl.ANY)] * 3,
            out_specs=pl.BlockSpec(memory_space=pltpu.VMEM),
            scratch_shapes=[
                pltpu.VMEM((C * D, G, part * K, J), bf16),
                pltpu.VMEM((GY, J, R2), bf16),
                pltpu.VMEM((K, R3), bf16),
                pltpu.VMEM((K, R3), f32),
                pltpu.VMEM((GZ, K, R3), f32),
                pltpu.VMEM((R3, 2 * GZ * K), bf16),
                pltpu.VMEM((C * D, R3 * part, R2), f32),
                pltpu.VMEM((C * D, GX, share // D, R2), bf16),
                pltpu.VMEM((C * D, GX, share // D, R2), bf16),
                pltpu.VMEM((G, N1 // G, lanes), f32),
                pltpu.VMEM((GX * G, N1 // G, lanes), f32),
                dma((C * D + 2,)),
                dma((C * D,)), dma((C * D,)),
                dma((GY,)), dma((GY,)),
                dma((GZ,)), dma((GZ,)),
                dma((C * D,)), dma((C * D,)),
                dma((1,)), dma((1,)),
                pltpu.SemaphoreType.REGULAR((GX - 1,)),
            ],
            compiler_params=pltpu.CompilerParams(
                collective_id=0, has_side_effects=True, vmem_limit_bytes=62 * 1024 * 1024),
        )(snapshot.reshape(S, NI * K, J), factor_two, factor_three).T

    placed = (P(None, "gx", "gz", "gy"), P("gy", None), P("gz", None))
    return jax.shard_map(
        per_device, mesh=mesh, in_specs=placed, out_specs=P("gx", ("gy", "gz")), check_vma=False
    )
```

```python
import functools

import jax
import jax.numpy as jnp
from jax import lax
from jax.experimental import pallas as pl
from jax.experimental.pallas import tpu as pltpu
from jax.sharding import PartitionSpec as P

MESH = pl.DeviceIdType.MESH
NT = (((1,), (1,)), ((), ()))


def kernel(dims, snap, f2, f3, out, rx, f2rx, f3raw, f3own, f3rx, mix, z32, tx2, rx2, g, rx4,
           local_sem, send1, recv1, sendf2, recvf2, sendf3, recvf3, send2, recv2, send4, recv4, line, spread2):
    GX, GY, GZ, S, C, D, H, NI, K, R3, N1, total = dims
    G = GY * GZ
    T, NI_, W = C * D, NI // D, N1 // G
    x, y, z = lax.axis_index("gx"), lax.axis_index("gy"), lax.axis_index("gz")
    me = y * GZ + z

    def plane(p):
        return {"gy": lax.div(p, GZ), "gz": lax.rem(p, GZ)}

    def plus(index, offset, size):
        return lax.rem(index + offset, size)

    def cells(p, t):
        return snap.at[lax.div(p, H) * C + t // D, pl.ds(t % D * NI_ * K, NI_ * K)]

    def remote(src, dst, send, recv, device):
        return pltpu.make_async_remote_copy(
            src_ref=src, dst_ref=dst, send_sem=send, recv_sem=recv, device_id=device, device_id_type=MESH)

    barrier = pltpu.get_barrier_semaphore()
    for o in range(1, GZ):
        pl.semaphore_signal(barrier, inc=1, device_id={"gz": plus(z, o, GZ)}, device_id_type=MESH)
    for o in range(1, GY):
        pl.semaphore_signal(barrier, inc=1, device_id={"gy": plus(y, o, GY)}, device_id_type=MESH)

    def neighbours(semaphore):
        @pl.when(x > 0)
        def _():
            pl.semaphore_signal(semaphore, inc=1, device_id={"gx": x - 1}, device_id_type=MESH)

        @pl.when(x < GX - 1)
        def _():
            pl.semaphore_signal(semaphore, inc=1, device_id={"gx": x + 1}, device_id_type=MESH)

    beside = jnp.where(x > 0, 1, 0) + jnp.where(x < GX - 1, 1, 0)
    neighbours(barrier)
    first = pltpu.make_async_copy(f3, f3raw, local_sem.at[T + 1])
    first.start()
    own = [pltpu.make_async_copy(cells(me, t), rx.at[t, me], local_sem.at[t]) for t in range(T)]
    own.append(pltpu.make_async_copy(f2, f2rx.at[y], local_sem.at[T]))
    for copy in own:
        copy.start()
    pl.semaphore_wait(barrier, GY - 1 + GZ - 1 + beside)

    far = sorted(range(GZ), key=lambda b: -min(b, GZ - b))

    near = [(0, b) for b in far if b] + [(a, 0) for a in range(1, GY)]
    cross = [(a, b) for a in reversed(range(1, GY)) for b in far if b]

    def spread(t, offsets):
        for a, b in offsets:
            place = {"gy": plus(y, a, GY), "gz": plus(z, b, GZ)}
            p = place["gy"] * GZ + place["gz"]
            remote(cells(p, t), rx.at[t, me], send1.at[t], recv1.at[t], place).start()

    for o in range(1, GY):
        pl.semaphore_signal(line.at[GX - 2], inc=1, device_id={"gy": plus(y, o, GY)}, device_id_type=MESH)
    J = f2.shape[0]
    Q = GX if J % (16 * GX) == 0 else 1
    mine = pl.ds(pl.multiple_of(x * (J // Q), J // Q), J // Q) if Q > 1 else pl.ds(0, J)
    early = [remote(f2.at[mine], f2rx.at[y, mine], sendf2.at[o], recvf2.at[o], {"gy": plus(y, o, GY)}) for o in range(1, GY)]
    for copy in early:
        copy.start()
    spread(0, near)
    pl.semaphore_wait(line.at[GX - 2], GY - 1)
    spread(0, cross)
    first.wait()
    f3own[...] = f3raw[...].astype(jnp.float32)
    sends = []
    for o in range(1, GZ):
        sends.append(remote(f3own, f3rx.at[z], sendf3.at[o], recvf3.at[o], {"gz": plus(z, o, GZ)}))
    for copy in sends:
        copy.start()
    sends.extend(early)
    for t in range(1, T):
        spread(t, cross + near)
    f3rx[z] = f3own[...]
    g[...] = jnp.zeros_like(g)

    for step in range(GX - 2):
        neighbours(line.at[step])
        pl.semaphore_wait(line.at[step], beside)

    for o in range(1, GY):
        q = plus(y, GY - o, GY)
        remote(f2.at[mine], f2rx.at[q, mine], sendf2.at[o], recvf2.at[o], {"gy": q}).wait_recv()
        for b in range(1, GX if Q > 1 else 1):
            copy = remote(f2rx.at[q, mine], f2rx.at[q, mine], spread2.at[o], spread2.at[GY + o], {"gx": plus(x, b, GX)})
            copy.start()
    for o in range(1, GY if Q > 1 else 1):
        rest = f2rx.at[plus(y, GY - o, GY), pl.ds(0, (GX - 1) * (J // Q))]
        remote(rest, rest, spread2.at[o], spread2.at[GY + o], {"gx": plus(x, 1, GX)}).wait_recv()
    own[T].wait()
    for o in range(1, GZ):
        q = plus(z, GZ - o, GZ)
        remote(f3own, f3rx.at[q], sendf3.at[o], recvf3.at[o], {"gz": q}).wait_recv()
    whole2 = jnp.concatenate([f2rx[b] for b in range(GY)], axis=0)
    if H > 1:
        R2 = whole2.shape[1]
        lanes = lax.div(lax.broadcasted_iota(jnp.int32, whole2.shape, 1), R2 // H)
        whole2 = jnp.where(lanes == lax.rem(me, H), whole2.astype(jnp.float32), 0.0).astype(jnp.bfloat16)
    whole3 = jnp.concatenate([f3rx[b] for b in range(GZ)] * 2, axis=0).astype(jnp.bfloat16)
    rows = lax.broadcasted_iota(jnp.int32, (R3, R3), 0)
    cols = lax.broadcasted_iota(jnp.int32, (R3, R3), 1)
    unit = jnp.where(rows == cols, 1.0, 0.0).astype(jnp.bfloat16)
    mix[...] = lax.dot_general(unit, whole3, NT, preferred_element_type=jnp.float32).astype(jnp.bfloat16)

    for t in range(T):
        own[t].wait()
        arrived = rx.at[t, pl.ds(0, G - 1)]
        remote(arrived, arrived, send1.at[t], recv1.at[t], plane(plus(me, 1, G))).wait_recv()
        second = []
        for b in range(GZ):
            wide = jnp.concatenate([rx[t, a * GZ + b] for a in range(GY)], axis=1)
            second.append(jnp.dot(wide, whole2, preferred_element_type=jnp.float32))
        for i in range(0, NI_, 2):
            pair = []
            for n in (i, i + 1):
                fibre = jnp.concatenate([block[n * K:(n + 1) * K] for block in second], axis=0)
                high = fibre.astype(jnp.bfloat16)
                low = (fibre - high.astype(jnp.float32)).astype(jnp.bfloat16)
                pair.append(jnp.concatenate([high, low], axis=0))
            both = jnp.dot(mix[...], jnp.concatenate(pair, axis=1), preferred_element_type=jnp.float32)
            R2 = both.shape[1] // 2
            z32[t, pl.ds(i, R3, stride=NI_), :] = both[:, :R2]
            z32[t, pl.ds(i + 1, R3, stride=NI_), :] = both[:, R2:]
        share = R3 // GX * NI_
        for b in range(GX):
            tx2[t, b] = z32[t, b * share:(b + 1) * share, :].astype(jnp.bfloat16)
        for o in range(1, GX):
            q = plus(x, o, GX)
            copy = remote(tx2.at[t, q], rx2.at[t, x], send2.at[t], recv2.at[t], {"gx": q})
            copy.start()
        rx2[t, x] = tx2[t, x]

    gram = None
    for c in range(C):
        for t in range(c * D, c * D + D):
            gathered = rx2.at[t, pl.ds(0, GX - 1)]
            remote(gathered, gathered, send2.at[t], recv2.at[t], {"gx": plus(x, 1, GX)}).wait_recv()
        blocks = [rx2[c * D + d, b].astype(jnp.float32) for b in range(GX) for d in range(D)]
        fibres = jnp.concatenate(
            [jnp.concatenate([block[r * NI_:(r + 1) * NI_] for block in blocks], axis=0) for r in range(R3 // GX)],
            axis=1).astype(jnp.bfloat16)
        term = lax.dot_general(fibres, fibres, NT, preferred_element_type=jnp.float32)
        gram = term if gram is None else gram + term

    for b in range(G):
        g[b, :, :N1] = gram[b * W:(b + 1) * W]
    flat, N = x * G + me, GX * G
    columns = [plus(me, b, G) for b in range(G)]
    places = [plane(p) for p in columns]
    for a in range(GX):
        dx = plus(x, a, GX)
        for b in range(1 if a == 0 else 0, G):
            remote(g.at[columns[b]], rx4.at[flat], send4.at[0], recv4.at[0], {"gx": dx, **places[b]}).start()
    rx4[flat] = g[me]
    for t in range(T):
        arrived = rx.at[t, pl.ds(0, G - 1)]
        remote(arrived, arrived, send1.at[t], recv1.at[t], plane(plus(me, 1, G))).wait_send()
        gathered = rx2.at[t, pl.ds(0, GX - 1)]
        remote(gathered, gathered, send2.at[t], recv2.at[t], {"gx": plus(x, 1, GX)}).wait_send()
    for copy in sends:
        copy.wait_send()
    for o in range(1, GY if Q > 1 else 1):
        rest = f2rx.at[plus(y, GY - o, GY), pl.ds(0, (GX - 1) * (J // Q))]
        remote(rest, rest, spread2.at[o], spread2.at[GY + o], {"gx": plus(x, 1, GX)}).wait_send()
    others = rx4.at[pl.ds(0, N - 1)]
    remote(others, others, send4.at[0], recv4.at[0], plane(plus(me, 1, G))).wait_recv()
    summed = jnp.sum(rx4[...], axis=0)
    lanes = summed.shape[1]
    summed = pltpu.roll(summed, lax.rem(lanes - NI * x, lanes), 1)
    out[...] = summed[:, :NI] / total
    remote(others, others, send4.at[0], recv4.at[0], plane(plus(me, 1, G))).wait_send()


def solution(mesh):
    GX, GY, GZ = (mesh.shape[name] for name in ("gx", "gy", "gz"))
    G = GY * GZ

    def per_device(snapshot, factor_two, factor_three):
        S, NI, K, J = snapshot.shape
        R2, R3 = factor_two.shape[1], factor_three.shape[1]
        N1 = NI * GX
        C, H = max(1, S // G), max(1, G // S)
        share = R3 // GX * NI
        lanes = -(-N1 // 128) * 128
        D = 2 if share % 32 == 0 else 1
        part = NI // D
        dims = (GX, GY, GZ, S, C, D, H, NI, K, R3, N1, float(R2 * R3 * S))
        dma = pltpu.SemaphoreType.DMA
        f32, bf16 = jnp.float32, jnp.bfloat16
        return pl.pallas_call(
            functools.partial(kernel, dims),
            out_shape=pltpu.VMEM((N1 // G, NI), f32),
            in_specs=[pl.BlockSpec(memory_space=pl.ANY)] * 3,
            out_specs=pl.BlockSpec(memory_space=pltpu.VMEM),
            scratch_shapes=[
                pltpu.VMEM((C * D, G, part * K, J), bf16),
                pltpu.VMEM((GY, J, R2), bf16),
                pltpu.VMEM((K, R3), bf16),
                pltpu.VMEM((K, R3), f32),
                pltpu.VMEM((GZ, K, R3), f32),
                pltpu.VMEM((R3, 2 * GZ * K), bf16),
                pltpu.VMEM((C * D, R3 * part, R2), f32),
                pltpu.VMEM((C * D, GX, share // D, R2), bf16),
                pltpu.VMEM((C * D, GX, share // D, R2), bf16),
                pltpu.VMEM((G, N1 // G, lanes), f32),
                pltpu.VMEM((GX * G, N1 // G, lanes), f32),
                dma((C * D + 2,)),
                dma((C * D,)), dma((C * D,)),
                dma((GY,)), dma((GY,)),
                dma((GZ,)), dma((GZ,)),
                dma((C * D,)), dma((C * D,)),
                dma((1,)), dma((1,)),
                pltpu.SemaphoreType.REGULAR((GX - 1,)),
                dma((2 * GY,)),
            ],
            compiler_params=pltpu.CompilerParams(
                collective_id=0, has_side_effects=True, vmem_limit_bytes=62 * 1024 * 1024),
        )(snapshot.reshape(S, NI * K, J), factor_two, factor_three).T

    placed = (P(None, "gx", "gz", "gy"), P("gy", None), P("gz", None))
    return jax.shard_map(
        per_device, mesh=mesh, in_specs=placed, out_specs=P("gx", ("gy", "gz")), check_vma=False
    )
```
